32 devices in a mesh: ctx: 8 (over z, x), head: 4 (over y, core).
Axes of the slice: x: 2, y: 2, z: 4, core: 2. Of those that a mesh axis runs over, the one named last changes fastest.
Arguments:
- queries: bfloat16 [1024, 2048], P('ctx', 'head'), may hold values from -120 to 120
- keys: bfloat16 [1024, 512], P('ctx', 'head'), may hold values from -4.5 to 4.5
- values: bfloat16 [1024, 512], P('ctx', 'head'), may hold values from -6 to 6
- segments: int32 [1024], replicated, may hold values from 0 to 2, never falling along the last dimension, each value on 1 to 512 neighbouring positions
- residual: bfloat16 [1024, 8192], P('ctx', 'head'), may hold values from -1.5 to 1.5
- out_weight: bfloat16 [2048, 8192], P('head'), may hold values from -1.5 to 1.5
Outputs:
- mixed: bfloat16 [1024, 8192], P('ctx', 'head')
The draws below stay inside these ranges and needn't reach their ends.
Inputs may be any that keep to these rules, and one draw needn't show every extreme that they name: `segments`: no document is longer than 512 positions.
All inputs are finite; a program needn't handle non-finite values.
Results may differ from the reference program's by a relative error of at most 0.015.
Values may be sent and summed in bfloat16 or wider, within the bound.
A program may use at most 128 MiB of HBM per device.

```python
import math
import jax
import jax.numpy as jnp
import numpy as np
from jax import lax

D = 8192
HD = 128
QH_DEV = 4
KV_HEADS = 4
Q_HEADS = 16
TOKENS = 1024
DOCMAX = 512
N_CTX = 8


def paired_draw(key):
    key_seed = jax.random.fold_in(key, 101)
    query_seed = jax.random.fold_in(key, 202)
    key_rows = jnp.clip(jax.random.normal(key_seed, (TOKENS, KV_HEADS * HD), jnp.float32), -4.5, 4.5)
    query_rows = jnp.clip(2.5 * jax.random.normal(query_seed, (TOKENS, Q_HEADS * HD), jnp.float32), -15.0, 15.0)
    return (query_rows, key_rows)


def draw_queries(key, part):
    return paired_draw(key)[0].astype(jnp.bfloat16)


def draw_keys(key, part):
    return paired_draw(key)[1].astype(jnp.bfloat16)


def shard_levels(stream_key, dims, pieces, least, largest):
    gain = 1.0
    for dim, shards_of in pieces:
        draws = jax.random.uniform(jax.random.fold_in(jax.random.fold_in(stream_key, 6), dim), (shards_of,), jnp.float32, least / len(pieces), largest / len(pieces))
        gain = gain * jnp.repeat(jnp.exp(draws), dims[dim] // shards_of).reshape((-1,) + (1,) * (len(dims) - 1 - dim))
    return gain


def split_up(count, total, reach, slope):
    loads = [(1 << 20) // math.isqrt(standing ** slope) + 1 for standing in range(2, count + 1)]
    surplus, given = total - reach - (count - 1), [1] * (count - 1)
    while surplus > 0:
        movable = [i for i in range(count - 1) if given[i] < reach]
        mass, remaining = sum([loads[i] for i in movable]), surplus
        for i in movable:
            extra = min(reach - given[i], max(1, remaining * loads[i] // mass), surplus)
            given[i] = given[i] + extra
            surplus = surplus - extra
    return np.array([reach] + given)


def ragged(stream_key, amount, total, bound, slope):
    if amount == 2:
        one = jax.random.randint(stream_key, (), max(1, total - bound), min(bound, total - 1) + 1)
        return jnp.stack([one, total - one])
    sizes = jnp.asarray(split_up(amount, total, bound, slope), jnp.int32)
    twos = (amount - 1) // 2
    giver, sink = sizes[1:1 + 2 * twos:2], sizes[2:2 + 2 * twos:2]
    slack = jnp.minimum(giver - 1, bound - sink)
    moved = jax.random.randint(jax.random.fold_in(stream_key, 1), (twos,), 0, 1 << 20) % (slack + 1)
    sizes = sizes.at[1:1 + 2 * twos:2].set(giver - moved).at[2:2 + 2 * twos:2].set(sink + moved)
    return sizes[jax.random.permutation(jax.random.fold_in(stream_key, 2), amount)]


def gaussian(stream_key, dims, scale, reach, pieces=(), kind=jnp.bfloat16):
    loudness = shard_levels(stream_key, dims, pieces, -0.22, 0.18) if pieces else 1.0
    result = jax.random.normal(stream_key, dims, jnp.float32) * scale * loudness
    return jnp.minimum(jnp.maximum(result, -reach), reach).astype(kind)


def setup_inputs(seed: int = 0) -> dict:
    arg_keys = jax.random.split(jax.random.key(seed), 7)
    queries = draw_queries(jax.random.fold_in(arg_keys[6], 71), 0)
    keys = draw_keys(jax.random.fold_in(arg_keys[6], 71), 0)
    values = gaussian(arg_keys[2], (TOKENS, KV_HEADS * HD), 1.0, 6.0, ((0, 8), (1, 4)))
    segments = jnp.searchsorted(jnp.cumsum(ragged(arg_keys[3], max(3, N_CTX // 8), TOKENS, DOCMAX, 2)), jnp.arange(TOKENS), side="right").astype(jnp.int32)
    residual = gaussian(arg_keys[4], (TOKENS, D), 0.25, 1.5, ((0, 8), (1, 4)))
    out_weight = gaussian(arg_keys[5], (Q_HEADS * HD, D), Q_HEADS ** -0.5, 1.5, ((0, 4),))
    return dict(queries=queries, keys=keys, values=values, segments=segments, residual=residual, out_weight=out_weight)


def reference(queries, keys, values, segments, residual, out_weight):
    block_rows = math.gcd(512, TOKENS)
    key_span = min(TOKENS, DOCMAX + block_rows)
    score_scale = 1.0 / math.sqrt(HD)
    query_offsets = jnp.arange(block_rows, dtype=jnp.int32)
    key_offsets = jnp.arange(key_span, dtype=jnp.int32)

    def attend_block(block_index):
        query_first = (block_index * block_rows).astype(jnp.int32)
        key_first = jnp.clip(query_first + block_rows - key_span, 0, TOKENS - key_span).astype(jnp.int32)
        query_block = lax.dynamic_slice_in_dim(queries, query_first, block_rows, 0).astype(jnp.float32)
        query_block = query_block.reshape(block_rows, KV_HEADS, QH_DEV, HD)
        key_block = lax.dynamic_slice_in_dim(keys, key_first, key_span, 0).astype(jnp.float32)
        key_block = key_block.reshape(key_span, KV_HEADS, HD)
        value_block = lax.dynamic_slice_in_dim(values, key_first, key_span, 0).astype(jnp.float32)
        value_block = value_block.reshape(key_span, KV_HEADS, HD)
        query_segment = lax.dynamic_slice_in_dim(segments, query_first, block_rows, 0)
        key_segment = lax.dynamic_slice_in_dim(segments, key_first, key_span, 0)
        visible = (query_segment[:, None] == key_segment[None, :]) & ((key_first + key_offsets)[None, :] <= (query_first + query_offsets)[:, None])
        scores = jnp.einsum('qhgd,khd->hgqk', query_block, key_block) * score_scale
        scores = jnp.where(visible[None, None], scores, -jnp.inf)
        top_score = lax.optimization_barrier(jnp.max(scores, axis=-1, keepdims=True))
        raw_weights = jnp.exp(scores - top_score)
        total = lax.optimization_barrier(jnp.sum(raw_weights, axis=-1))
        weights = lax.optimization_barrier(raw_weights.astype(jnp.bfloat16)).astype(jnp.float32)
        summed = jnp.einsum('hgqk,khd->qhgd', weights, value_block)
        attended = summed / jnp.transpose(total, (2, 0, 1))[..., None]
        return attended.reshape(block_rows, Q_HEADS * HD).astype(jnp.bfloat16)
    attended = lax.map(attend_block, jnp.arange(TOKENS // block_rows, dtype=jnp.int32))
    attended = attended.reshape(TOKENS, Q_HEADS * HD)
    projected = jnp.dot(attended, out_weight, preferred_element_type=jnp.float32)
    return (residual.astype(jnp.float32) + projected).astype(jnp.bfloat16)
```

```python
import functools
import math

import jax
import jax.numpy as jnp
from jax import lax
from jax.experimental import pallas as pl
from jax.experimental.pallas import tpu as pltpu
from jax.sharding import PartitionSpec as P

HD = 128
MESH = pl.DeviceIdType.MESH


def each(items, body):
    if len(items) <= 8:
        for item in items:
            body(item)
    elif len(items) > 0:

        @pl.loop(0, len(items))
        def _(step):
            body(items.start + step * items.step)


def kernel(
    dims,
    q_ref,
    k_ref,
    v_ref,
    seg_ref,
    res_hbm,
    w_hbm,
    out_ref,
    kv,
    w,
    tx_pair,
    rx_pair,
    tx_far,
    rx_far,
    acc,
    res,
    kv_send,
    kv_pass,
    kv_recv,
    pair_send,
    pair_recv,
    far_send,
    far_recv,
    w_sem,
    res_sem,
):
    n_ctx, n_head, far, chunks, key_blocks = dims
    rows, q_cols = q_ref.shape
    group = q_cols // HD
    out_cols = out_ref.shape[1]
    width = out_cols // chunks
    pairs = n_head // 2
    me = lax.axis_index("ctx")
    head = lax.axis_index("head")
    side = lax.rem(head, 2)
    pair = lax.div(head, 2)
    mate = head + 1 - 2 * side
    odd = lax.rem(me, 2)
    ctx_mate = me + 1 - 2 * odd

    def pair_at(j):
        return lax.rem(pair + j, pairs)

    order = [j % pairs for j in range(1, pairs + 1)]

    def w_copy(slot, j, other, c):
        part = 2 * pair_at(j) + (1 - side if other else side)
        start = pl.multiple_of(part * out_cols + c * width, 128)
        return pltpu.make_async_copy(
            w_hbm.at[:, pl.ds(start, width)], w.at[slot], w_sem.at[slot]
        )

    w_copies = {}
    for j in order:
        for other in (True, False):
            for c in range(chunks):
                slot = len(w_copies)
                w_copies[j, other, c] = (slot, w_copy(slot, j, other, c))
    for _, copy in w_copies.values():
        copy.start()
    res_copy = pltpu.make_async_copy(res_hbm, res, res_sem)
    res_copy.start()

    barrier = pltpu.get_barrier_semaphore()

    def greet(ctx, hd):
        pl.semaphore_signal(barrier, inc=1, device_id=(ctx, hd), device_id_type=MESH)

    def greet_ctx(k):
        @pl.when(me + k < n_ctx)
        def _():
            greet(me + k, head)

        @pl.when(me - k >= 0)
        def _():
            greet(me - k, head)

    evens = range(2, far + 1, 2)
    each(evens, greet_ctx)
    greet(ctx_mate, head)
    greet(me, mate)
    for j in range(1, pairs):
        greet(me, 2 * pair_at(j) + side)
    kv[0, 0] = k_ref[...]
    kv[0, 1] = v_ref[...]

    def clear(k):
        @pl.when(me - k < 0)
        def _():
            kv[k] = jnp.zeros(kv.shape[1:], kv.dtype)

    each(range(1, far + 1), clear)
    ahead = jnp.minimum(lax.div(n_ctx - 1 - me, 2), far // 2)
    behind = jnp.minimum(lax.div(me, 2), far // 2)
    pl.semaphore_wait(barrier, ahead + behind + 1 + pairs)

    def direct(k):
        return pltpu.make_async_remote_copy(
            src_ref=kv.at[0],
            dst_ref=kv.at[k],
            send_sem=kv_send.at[k],
            recv_sem=kv_recv.at[k],
            device_id=(me + k, head),
            device_id_type=MESH,
        )

    def passed(k, lands):
        return pltpu.make_async_remote_copy(
            src_ref=kv.at[k],
            dst_ref=kv.at[lands],
            send_sem=kv_pass.at[k],
            recv_sem=kv_recv.at[lands],
            device_id=(ctx_mate, head),
            device_id_type=MESH,
        )

    def arrival(k):
        return pltpu.make_async_remote_copy(
            src_ref=kv.at[0],
            dst_ref=kv.at[k],
            send_sem=kv_send.at[k],
            recv_sem=kv_recv.at[k],
            device_id=(ctx_mate, head),
            device_id_type=MESH,
        )

    def send_direct(k):
        @pl.when(me + k < n_ctx)
        def _():
            direct(k).start()

    each(evens, send_direct)

    @pl.when(odd == 0)
    def _():
        passed(0, 1).start()

    def receive_even(k):
        @pl.when(me - k >= 0)
        def _():
            arrival(k).wait_recv()

            @pl.when(odd == 1)
            def _():
                passed(k, k - 1).start()

            @pl.when((odd == 0) & (k < far))
            def _():
                passed(k, jnp.minimum(k + 1, far)).start()

    each(evens, receive_even)

    def receive_odd(k):
        @pl.when(me - k >= 0)
        def _():
            arrival(k).wait_recv()

    each(range(1, far + 1, 2), receive_odd)

    row = lax.broadcasted_iota(jnp.int32, (rows, rows), 0)
    lane = lax.broadcasted_iota(jnp.int32, (rows, rows), 1)
    own_segment = seg_ref[pl.ds(me, 1), :].astype(jnp.float32)
    q_segment = jnp.sum(jnp.where(row == lane, own_segment, 0.0), axis=1, keepdims=True)
    queries = jnp.concatenate([q_ref[:, g * HD : (g + 1) * HD] for g in range(group)], axis=0)
    scale = 1.0 / math.sqrt(HD)

    def attend(step, state):
        best, total, summed = state
        first = step * key_blocks
        visible = []
        for b in range(key_blocks):
            k = first + b
            segment = seg_ref[pl.ds(jnp.maximum(me - k, 0), 1), :].astype(jnp.float32)
            near = (lane - k * rows <= row) & (me - k >= 0)
            visible.append((q_segment == segment) & near)
        visible = jnp.concatenate(
            [jnp.where(v, 0.0, -jnp.inf) for v in visible], axis=1
        )
        visible = jnp.concatenate([visible] * group, axis=0)
        block = kv[pl.ds(first, key_blocks)]
        keys = block[:, 0].reshape(key_blocks * rows, HD)
        values = block[:, 1].reshape(key_blocks * rows, HD)
        scores = lax.dot_general(
            queries, keys, (((1,), (1,)), ((), ())), preferred_element_type=jnp.float32
        )
        scores = scores * scale + visible
        best_new = jnp.maximum(best, jnp.max(scores, axis=1, keepdims=True))
        weights = jnp.exp(scores - best_new)
        shrink = jnp.exp(best - best_new)
        total = total * shrink + jnp.sum(weights, axis=1, keepdims=True)
        summed = summed * shrink + jnp.dot(
            weights.astype(jnp.bfloat16), values, preferred_element_type=jnp.float32
        )
        return best_new, total, summed

    state = (
        jnp.full((group * rows, 1), -1e30, jnp.float32),
        jnp.zeros((group * rows, 1), jnp.float32),
        jnp.zeros((group * rows, HD), jnp.float32),
    )
    steps = (far + 1) // key_blocks
    if steps == 1:
        state = attend(0, state)
    else:
        state = lax.fori_loop(0, steps, attend, state)
    _, total, summed = state
    attended = (summed / total).astype(jnp.bfloat16)
    attended = jnp.concatenate(
        [attended[g * rows : (g + 1) * rows] for g in range(group)], axis=1
    )

    def project(j, other, c):
        slot, copy = w_copies[j, other, c]
        copy.wait()
        return jnp.dot(attended, w[slot], preferred_element_type=jnp.float32)

    def to_mate(i):
        return pltpu.make_async_remote_copy(
            src_ref=tx_pair.at[i],
            dst_ref=rx_pair.at[i],
            send_sem=pair_send.at[i],
            recv_sem=pair_recv.at[i],
            device_id=(me, mate),
            device_id_type=MESH,
        )

    def to_far(j, c):
        i = (j - 1) * chunks + c
        return pltpu.make_async_remote_copy(
            src_ref=tx_far.at[i],
            dst_ref=rx_far.at[i],
            send_sem=far_send.at[i],
            recv_sem=far_recv.at[i],
            device_id=(me, 2 * pair_at(j) + side),
            device_id_type=MESH,
        )

    for j in order:
        for c in range(chunks):
            i = j * chunks + c
            tx_pair[i] = project(j, True, c).astype(jnp.bfloat16)
            to_mate(i).start()
        for c in range(chunks):
            i = j * chunks + c
            mine = project(j, False, c)
            to_mate(i).wait_recv()
            mine = mine + rx_pair[i].astype(jnp.float32)
            if j > 0:
                tx_far[(j - 1) * chunks + c] = mine.astype(jnp.bfloat16)
                to_far(j, c).start()
            else:
                acc[c] = mine
    res_copy.wait()
    for c in range(chunks):
        columns = slice(c * width, (c + 1) * width)
        whole = acc[c] + res[:, columns].astype(jnp.float32)
        for j in range(1, pairs):
            to_far(j, c).wait_recv()
            whole = whole + rx_far[(j - 1) * chunks + c].astype(jnp.float32)
        out_ref[:, columns] = whole.astype(out_ref.dtype)

    for i in range(pairs * chunks):
        to_mate(i).wait_send()
    for j in range(1, pairs):
        for c in range(chunks):
            to_far(j, c).wait_send()

    def sent(k):
        @pl.when(me + k < n_ctx)
        def _():
            direct(k).wait_send()

        @pl.when((me - k >= 0) & ((odd == 1) | (k < far)))
        def _():
            passed(k, k - 1).wait_send()

    each(evens, sent)

    @pl.when(odd == 0)
    def _():
        passed(0, 1).wait_send()


def local(queries, keys, values, segments, residual, out_weight):
    n_ctx, n_head = lax.axis_size("ctx"), lax.axis_size("head")
    rows, out_cols = residual.shape
    depth = out_weight.shape[0]
    far = n_ctx // 2
    pairs = n_head // 2
    width = min(512, out_cols)
    chunks = out_cols // width
    key_blocks = max(b for b in range(1, 9) if (far + 1) % b == 0)
    vmem = pl.BlockSpec(memory_space=pltpu.VMEM)
    hbm = pl.BlockSpec(memory_space=pl.ANY)
    bf16 = jnp.bfloat16
    far_slots = max(1, (pairs - 1) * chunks)
    return pl.pallas_call(
        functools.partial(kernel, (n_ctx, n_head, far, chunks, key_blocks)),
        out_shape=jax.ShapeDtypeStruct((rows, out_cols), bf16),
        in_specs=[vmem, vmem, vmem, vmem, hbm, hbm],
        out_specs=vmem,
        scratch_shapes=[
            pltpu.VMEM((far + 1, 2, rows, HD), bf16),
            pltpu.VMEM((n_head * chunks, depth, width), bf16),
            pltpu.VMEM((pairs * chunks, rows, width), bf16),
            pltpu.VMEM((pairs * chunks, rows, width), bf16),
            pltpu.VMEM((far_slots, rows, width), bf16),
            pltpu.VMEM((far_slots, rows, width), bf16),
            pltpu.VMEM((chunks, rows, width), jnp.float32),
            pltpu.VMEM((rows, out_cols), bf16),
            pltpu.SemaphoreType.DMA((far + 1,)),
            pltpu.SemaphoreType.DMA((far + 1,)),
            pltpu.SemaphoreType.DMA((far + 1,)),
            pltpu.SemaphoreType.DMA((pairs * chunks,)),
            pltpu.SemaphoreType.DMA((pairs * chunks,)),
            pltpu.SemaphoreType.DMA((far_slots,)),
            pltpu.SemaphoreType.DMA((far_slots,)),
            pltpu.SemaphoreType.DMA((n_head * chunks,)),
            pltpu.SemaphoreType.DMA,
        ],
        compiler_params=pltpu.CompilerParams(
            collective_id=0, has_side_effects=True, vmem_limit_bytes=56 * 1024 * 1024
        ),
    )(queries, keys, values, segments.reshape(n_ctx, rows), residual, out_weight)


def solution(mesh):
    placed = (
        P("ctx", "head"),
        P("ctx", "head"),
        P("ctx", "head"),
        P(),
        P("ctx", "head"),
        P("head", None),
    )
    return jax.shard_map(
        local, mesh=mesh, in_specs=placed, out_specs=P("ctx", "head"), check_vma=False
    )
```

```python
import functools
import math

import jax
import jax.numpy as jnp
from jax import lax
from jax.experimental import pallas as pl
from jax.experimental.pallas import tpu as pltpu
from jax.sharding import PartitionSpec as P

HD = 128
MESH = pl.DeviceIdType.MESH


def each(items, body):
    if len(items) <= 8:
        for item in items:
            body(item)
    elif len(items) > 0:

        @pl.loop(0, len(items))
        def _(step):
            body(items.start + step * items.step)


def fold(items, body, state):
    if len(items) <= 8:
        for item in items:
            state = body(item, state)
        return state
    return lax.fori_loop(
        0, len(items), lambda step, s: body(items.start + step * items.step, s), state
    )


def kernel(
    dims,
    q_hbm,
    k_hbm,
    v_hbm,
    seg_hbm,
    res_hbm,
    w_hbm,
    out_hbm,
    q_ref,
    seg_ref,
    kv,
    w,
    tx_pair,
    rx_pair,
    tx_far,
    rx_far,
    acc,
    res,
    kv_send,
    kv_pass,
    kv_recv,
    pair_send,
    pair_recv,
    far_send,
    far_recv,
    w_sem,
    res_sem,
    out_sem,
    in_sem,
):
    n_ctx, n_head, far, chunks = dims
    rows, q_cols = q_ref.shape
    group = q_cols // HD
    out_cols = out_hbm.shape[1]
    width = out_cols // chunks
    pairs = n_head // 2
    me = lax.axis_index("ctx")
    head = lax.axis_index("head")
    side = lax.rem(head, 2)
    pair = lax.div(head, 2)
    mate = head + 1 - 2 * side
    odd = lax.rem(me, 2)
    ctx_mate = me + 1 - 2 * odd

    def pair_at(j):
        return lax.rem(pair + j, pairs)

    barrier = pltpu.get_barrier_semaphore()

    def greet(ctx, hd):
        pl.semaphore_signal(barrier, inc=1, device_id=(ctx, hd), device_id_type=MESH)

    def greet_ctx(k):
        @pl.when(me + k < n_ctx)
        def _():
            greet(me + k, head)

        @pl.when(me - k >= 0)
        def _():
            greet(me - k, head)

    evens = range(2, far + 1, 2)
    greet_ctx(2)
    greet(ctx_mate, head)
    greet(me, mate)
    for j in range(1, pairs):
        greet(me, 2 * pair_at(j) + side)
    inputs = [
        pltpu.make_async_copy(source, target, in_sem.at[i])
        for i, (source, target) in enumerate(
            [
                (k_hbm, kv.at[0, 0]),
                (v_hbm, kv.at[0, 1]),
                (q_hbm, q_ref),
                (seg_hbm, seg_ref),
            ]
        )
    ]
    for copy in inputs:
        copy.start()

    order = [j % pairs for j in range(1, pairs + 1)]

    def w_copy(slot, j, other, c):
        part = 2 * pair_at(j) + (1 - side if other else side)
        start = pl.multiple_of(part * out_cols + c * width, 128)
        return pltpu.make_async_copy(
            w_hbm.at[:, pl.ds(start, width)], w.at[slot], w_sem.at[slot]
        )

    w_copies = {}
    for j in order:
        for c in range(chunks):
            for other in (True, False):
                slot = len(w_copies)
                w_copies[j, other, c] = (slot, w_copy(slot, j, other, c))
    for _, copy in w_copies.values():
        copy.start()
    res_copy = pltpu.make_async_copy(res_hbm, res, res_sem)
    res_copy.start()

    def clear(k):
        @pl.when(me - k < 0)
        def _():
            kv[k] = jnp.zeros(kv.shape[1:], kv.dtype)

    each(range(1, far + 1), clear)
    ahead = jnp.where(me + 2 < n_ctx, 1, 0)
    behind = jnp.where(me - 2 >= 0, 1, 0)
    pl.semaphore_wait(barrier, ahead + behind + 1 + pairs)

    inputs[0].wait()
    inputs[1].wait()

    def direct(k):
        return pltpu.make_async_remote_copy(
            src_ref=kv.at[k - 2],
            dst_ref=kv.at[k],
            send_sem=kv_send.at[k],
            recv_sem=kv_recv.at[k],
            device_id=(me + 2, head),
            device_id_type=MESH,
        )

    def passed(k, lands):
        return pltpu.make_async_remote_copy(
            src_ref=kv.at[k],
            dst_ref=kv.at[lands],
            send_sem=kv_pass.at[k],
            recv_sem=kv_recv.at[lands],
            device_id=(ctx_mate, head),
            device_id_type=MESH,
        )

    def arrival(k):
        return pltpu.make_async_remote_copy(
            src_ref=kv.at[0],
            dst_ref=kv.at[k],
            send_sem=kv_send.at[k],
            recv_sem=kv_recv.at[k],
            device_id=(ctx_mate, head),
            device_id_type=MESH,
        )

    @pl.when(me + 2 < n_ctx)
    def _():
        direct(2).start()

    @pl.when(odd == 0)
    def _():
        passed(0, 1).start()

    inputs[2].wait()
    inputs[3].wait()
    row = lax.broadcasted_iota(jnp.int32, (rows, rows), 0)
    lane = lax.broadcasted_iota(jnp.int32, (rows, rows), 1)
    own_segment = seg_ref[pl.ds(me, 1), :].astype(jnp.float32)
    q_segment = jnp.sum(jnp.where(row == lane, own_segment, 0.0), axis=1, keepdims=True)
    queries = jnp.concatenate([q_ref[:, g * HD : (g + 1) * HD] for g in range(group)], axis=0)
    scale = 1.0 / math.sqrt(HD)

    def attend(k, state):
        best, total, summed = state
        segment = seg_ref[pl.ds(jnp.maximum(me - k, 0), 1), :].astype(jnp.float32)
        near = (lane - k * rows <= row) & (me - k >= 0)
        visible = jnp.where((q_segment == segment) & near, 0.0, -jnp.inf)
        visible = jnp.concatenate([visible] * group, axis=0)
        keys = kv[k, 0]
        values = kv[k, 1]
        scores = lax.dot_general(
            queries, keys, (((1,), (1,)), ((), ())), preferred_element_type=jnp.float32
        )
        scores = scores * scale + visible
        best_new = jnp.maximum(best, jnp.max(scores, axis=1, keepdims=True))
        weights = jnp.exp(scores - best_new)
        shrink = jnp.exp(best - best_new)
        total = total * shrink + jnp.sum(weights, axis=1, keepdims=True)
        summed = summed * shrink + jnp.dot(
            weights.astype(jnp.bfloat16), values, preferred_element_type=jnp.float32
        )
        return best_new, total, summed

    state = (
        jnp.full((group * rows, 1), -1e30, jnp.float32),
        jnp.zeros((group * rows, 1), jnp.float32),
        jnp.zeros((group * rows, HD), jnp.float32),
    )
    state = attend(0, state)

    def take_even(k, state):
        @pl.when(me - k >= 0)
        def _():
            arrival(k).wait_recv()

            @pl.when((me + 2 < n_ctx) & (k < far))
            def _():
                direct(jnp.minimum(k + 2, far)).start()

            @pl.when(odd == 1)
            def _():
                passed(k, k - 1).start()

            @pl.when((odd == 0) & (k < far))
            def _():
                passed(k, jnp.minimum(k + 1, far)).start()

        return attend(k, state)

    def take_odd(k, state):
        @pl.when(me - k >= 0)
        def _():
            arrival(k).wait_recv()

        return attend(k, state)

    state = fold(evens, take_even, state)
    state = fold(range(1, far + 1, 2), take_odd, state)
    _, total, summed = state
    attended = (summed / total).astype(jnp.bfloat16)
    attended = jnp.concatenate(
        [attended[g * rows : (g + 1) * rows] for g in range(group)], axis=1
    )

    def project(j, other, c):
        slot, copy = w_copies[j, other, c]
        copy.wait()
        return jnp.dot(attended, w[slot], preferred_element_type=jnp.float32)

    def to_mate(i):
        return pltpu.make_async_remote_copy(
            src_ref=tx_pair.at[i],
            dst_ref=rx_pair.at[i],
            send_sem=pair_send.at[i],
            recv_sem=pair_recv.at[i],
            device_id=(me, mate),
            device_id_type=MESH,
        )

    def to_far(j, c):
        i = (j - 1) * chunks + c
        return pltpu.make_async_remote_copy(
            src_ref=tx_far.at[i],
            dst_ref=rx_far.at[i],
            send_sem=far_send.at[i],
            recv_sem=far_recv.at[i],
            device_id=(me, 2 * pair_at(j) + side),
            device_id_type=MESH,
        )

    lag = min(2, chunks)
    for j in order:
        for t in range(chunks + lag):
            if t < chunks:
                i = j * chunks + t
                tx_pair[i] = project(j, True, t).astype(jnp.bfloat16)
                to_mate(i).start()
            if t < lag:
                continue
            c = t - lag
            i = j * chunks + c
            mine = project(j, False, c)
            to_mate(i).wait_recv()
            mine = mine + rx_pair[i].astype(jnp.float32)
            if j > 0:
                tx_far[(j - 1) * chunks + c] = mine.astype(jnp.bfloat16)
                to_far(j, c).start()
            else:
                acc[c] = mine
    res_copy.wait()
    out_copies = []
    for c in range(chunks):
        columns = slice(c * width, (c + 1) * width)
        whole = acc[c] + res[:, columns].astype(jnp.float32)
        for j in range(1, pairs):
            to_far(j, c).wait_recv()
            whole = whole + rx_far[(j - 1) * chunks + c].astype(jnp.float32)
        res[:, columns] = whole.astype(res.dtype)
        out_copies.append(
            pltpu.make_async_copy(
                res.at[:, columns], out_hbm.at[:, columns], out_sem.at[c]
            )
        )
        out_copies[c].start()

    for copy in out_copies:
        copy.wait()
    for i in range(pairs * chunks):
        to_mate(i).wait_send()
    for j in range(1, pairs):
        for c in range(chunks):
            to_far(j, c).wait_send()

    def sent(k):
        @pl.when((me + 2 < n_ctx) & (me - (k - 2) >= 0))
        def _():
            direct(k).wait_send()

        @pl.when((me - k >= 0) & ((odd == 1) | (k < far)))
        def _():
            passed(k, k - 1).wait_send()

    each(evens, sent)

    @pl.when(odd == 0)
    def _():
        passed(0, 1).wait_send()


def local(queries, keys, values, segments, residual, out_weight):
    n_ctx, n_head = lax.axis_size("ctx"), lax.axis_size("head")
    rows, out_cols = residual.shape
    depth = out_weight.shape[0]
    far = n_ctx // 2
    pairs = n_head // 2
    width = min(512, out_cols)
    chunks = out_cols // width
    hbm = pl.BlockSpec(memory_space=pl.ANY)
    bf16 = jnp.bfloat16
    far_slots = max(1, (pairs - 1) * chunks)
    return pl.pallas_call(
        functools.partial(kernel, (n_ctx, n_head, far, chunks)),
        out_shape=jax.ShapeDtypeStruct((rows, out_cols), bf16),
        in_specs=[hbm] * 6,
        out_specs=hbm,
        scratch_shapes=[
            pltpu.VMEM(queries.shape, bf16),
            pltpu.VMEM((n_ctx, rows), jnp.int32),
            pltpu.VMEM((far + 1, 2, rows, HD), bf16),
            pltpu.VMEM((n_head * chunks, depth, width), bf16),
            pltpu.VMEM((pairs * chunks, rows, width), bf16),
            pltpu.VMEM((pairs * chunks, rows, width), bf16),
            pltpu.VMEM((far_slots, rows, width), bf16),
            pltpu.VMEM((far_slots, rows, width), bf16),
            pltpu.VMEM((chunks, rows, width), jnp.float32),
            pltpu.VMEM((rows, out_cols), bf16),
            pltpu.SemaphoreType.DMA((far + 1,)),
            pltpu.SemaphoreType.DMA((far + 1,)),
            pltpu.SemaphoreType.DMA((far + 1,)),
            pltpu.SemaphoreType.DMA((pairs * chunks,)),
            pltpu.SemaphoreType.DMA((pairs * chunks,)),
            pltpu.SemaphoreType.DMA((far_slots,)),
            pltpu.SemaphoreType.DMA((far_slots,)),
            pltpu.SemaphoreType.DMA((n_head * chunks,)),
            pltpu.SemaphoreType.DMA,
            pltpu.SemaphoreType.DMA((chunks,)),
            pltpu.SemaphoreType.DMA((4,)),
        ],
        compiler_params=pltpu.CompilerParams(
            collective_id=0, has_side_effects=True, vmem_limit_bytes=56 * 1024 * 1024
        ),
    )(queries, keys, values, segments.reshape(n_ctx, rows), residual, out_weight)


def solution(mesh):
    placed = (
        P("ctx", "head"),
        P("ctx", "head"),
        P("ctx", "head"),
        P(),
        P("ctx", "head"),
        P("head", None),
    )
    return jax.shard_map(
        local, mesh=mesh, in_specs=placed, out_specs=P("ctx", "head"), check_vma=False
    )
```

```python
import functools
import math

import jax
import jax.numpy as jnp
from jax import lax
from jax.experimental import pallas as pl
from jax.experimental.pallas import tpu as pltpu
from jax.sharding import PartitionSpec as P

HD = 128
MESH = pl.DeviceIdType.MESH


def each(items, body):
    if len(items) <= 8:
        for item in items:
            body(item)
    elif len(items) > 0:

        @pl.loop(0, len(items))
        def _(step):
            body(items.start + step * items.step)


def fold(items, body, state):
    if len(items) <= 8:
        for item in items:
            state = body(item, state)
        return state
    return lax.fori_loop(
        0, len(items), lambda step, s: body(items.start + step * items.step, s), state
    )


def kernel(
    dims,
    q_hbm,
    k_hbm,
    v_hbm,
    seg_hbm,
    res_hbm,
    w_hbm,
    out_hbm,
    q_ref,
    seg_ref,
    kv,
    w,
    tx_pair,
    rx_pair,
    tx_far,
    rx_far,
    acc,
    res,
    kv_send,
    kv_pass,
    kv_recv,
    pair_send,
    pair_recv,
    far_send,
    far_recv,
    w_sem,
    res_sem,
    out_sem,
    in_sem,
):
    n_ctx, n_head, far, chunks = dims
    rows, q_cols = q_ref.shape
    group = q_cols // HD
    out_cols = out_hbm.shape[1]
    width = out_cols // chunks
    pairs = n_head // 2
    me = lax.axis_index("ctx")
    head = lax.axis_index("head")
    side = lax.rem(head, 2)
    pair = lax.div(head, 2)
    mate = head + 1 - 2 * side
    odd = lax.rem(me, 2)
    ctx_mate = me + 1 - 2 * odd

    def pair_at(j):
        return lax.rem(pair + j, pairs)

    barrier = pltpu.get_barrier_semaphore()

    def greet(ctx, hd):
        pl.semaphore_signal(barrier, inc=1, device_id=(ctx, hd), device_id_type=MESH)

    def greet_ctx(k):
        @pl.when(me + k < n_ctx)
        def _():
            greet(me + k, head)

        @pl.when(me - k >= 0)
        def _():
            greet(me - k, head)

    evens = range(2, far + 1, 2)
    greet_ctx(2)
    greet(ctx_mate, head)
    greet(me, mate)
    for j in range(1, pairs):
        greet(me, 2 * pair_at(j) + side)
    inputs = [
        pltpu.make_async_copy(source, target, in_sem.at[i])
        for i, (source, target) in enumerate(
            [
                (k_hbm, kv.at[0, 0]),
                (v_hbm, kv.at[0, 1]),
                (q_hbm, q_ref),
                (seg_hbm, seg_ref),
            ]
        )
    ]
    for copy in inputs:
        copy.start()

    order = [j % pairs for j in range(1, pairs + 1)]

    def w_copy(slot, j, other, c):
        part = 2 * pair_at(j) + (1 - side if other else side)
        start = pl.multiple_of(part * out_cols + c * width, 128)
        return pltpu.make_async_copy(
            w_hbm.at[:, pl.ds(start, width)], w.at[slot], w_sem.at[slot]
        )

    w_copies = {}
    for j in order:
        for c in range(chunks):
            for other in (True, False):
                slot = len(w_copies)
                w_copies[j, other, c] = (slot, w_copy(slot, j, other, c))
    res_copy = pltpu.make_async_copy(res_hbm, res, res_sem)

    def clear(k):
        @pl.when(me - k < 0)
        def _():
            kv[k] = jnp.zeros(kv.shape[1:], kv.dtype)

    each(range(1, far + 1), clear)
    ahead = jnp.where(me + 2 < n_ctx, 1, 0)
    behind = jnp.where(me - 2 >= 0, 1, 0)
    pl.semaphore_wait(barrier, ahead + behind + 1 + pairs)

    inputs[0].wait()
    inputs[1].wait()

    def direct_part(p, k):
        return pltpu.make_async_remote_copy(
            src_ref=kv.at[k - 2, p],
            dst_ref=kv.at[k, p],
            send_sem=kv_send.at[k, p],
            recv_sem=kv_recv.at[k, p],
            device_id=(me + 2, head),
            device_id_type=MESH,
        )

    def passed_part(p, k, lands):
        return pltpu.make_async_remote_copy(
            src_ref=kv.at[k, p],
            dst_ref=kv.at[lands, p],
            send_sem=kv_pass.at[k, p],
            recv_sem=kv_recv.at[lands, p],
            device_id=(ctx_mate, head),
            device_id_type=MESH,
        )

    def arrival_part(p, k):
        return pltpu.make_async_remote_copy(
            src_ref=kv.at[0, p],
            dst_ref=kv.at[k, p],
            send_sem=kv_send.at[k, p],
            recv_sem=kv_recv.at[k, p],
            device_id=(ctx_mate, head),
            device_id_type=MESH,
        )

    def both(make, *args):
        return [make(p, *args) for p in range(2)]

    @pl.when(me + 2 < n_ctx)
    def _():
        for copy in both(direct_part, 2):
            copy.start()

    @pl.when(odd == 0)
    def _():
        for copy in both(passed_part, 0, 1):
            copy.start()

    for _, copy in w_copies.values():
        copy.start()
    res_copy.start()

    inputs[2].wait()
    inputs[3].wait()
    row = lax.broadcasted_iota(jnp.int32, (rows, rows), 0)
    lane = lax.broadcasted_iota(jnp.int32, (rows, rows), 1)
    own_segment = seg_ref[pl.ds(me, 1), :].astype(jnp.float32)
    q_segment = jnp.sum(jnp.where(row == lane, own_segment, 0.0), axis=1, keepdims=True)
    queries = jnp.concatenate([q_ref[:, g * HD : (g + 1) * HD] for g in range(group)], axis=0)
    scale = 1.0 / math.sqrt(HD)

    def attend(k, state):
        best, total, summed = state
        segment = seg_ref[pl.ds(jnp.maximum(me - k, 0), 1), :].astype(jnp.float32)
        near = (lane - k * rows <= row) & (me - k >= 0)
        visible = jnp.where((q_segment == segment) & near, 0.0, -jnp.inf)
        visible = jnp.concatenate([visible] * group, axis=0)
        keys = kv[k, 0]
        values = kv[k, 1]
        scores = lax.dot_general(
            queries, keys, (((1,), (1,)), ((), ())), preferred_element_type=jnp.float32
        )
        scores = scores * scale + visible
        best_new = jnp.maximum(best, jnp.max(scores, axis=1, keepdims=True))
        weights = jnp.exp(scores - best_new)
        shrink = jnp.exp(best - best_new)
        total = total * shrink + jnp.sum(weights, axis=1, keepdims=True)
        summed = summed * shrink + jnp.dot(
            weights.astype(jnp.bfloat16), values, preferred_element_type=jnp.float32
        )
        return best_new, total, summed

    state = (
        jnp.full((group * rows, 1), -1e30, jnp.float32),
        jnp.zeros((group * rows, 1), jnp.float32),
        jnp.zeros((group * rows, HD), jnp.float32),
    )
    state = attend(0, state)

    def take_even(k, state):
        @pl.when(me - k >= 0)
        def _():
            for p in range(2):
                arrival_part(p, k).wait_recv()

                @pl.when((me + 2 < n_ctx) & (k < far))
                def _():
                    direct_part(p, jnp.minimum(k + 2, far)).start()

                @pl.when(odd == 1)
                def _():
                    passed_part(p, k, k - 1).start()

                @pl.when((odd == 0) & (k < far))
                def _():
                    passed_part(p, k, jnp.minimum(k + 1, far)).start()

        return attend(k, state)

    def take_odd(k, state):
        @pl.when(me - k >= 0)
        def _():
            for copy in both(arrival_part, k):
                copy.wait_recv()

        return attend(k, state)

    state = fold(evens, take_even, state)
    state = fold(range(1, far + 1, 2), take_odd, state)
    _, total, summed = state
    attended = (summed / total).astype(jnp.bfloat16)
    attended = jnp.concatenate(
        [attended[g * rows : (g + 1) * rows] for g in range(group)], axis=1
    )

    def project(j, other, c):
        slot, copy = w_copies[j, other, c]
        copy.wait()
        return jnp.dot(attended, w[slot], preferred_element_type=jnp.float32)

    def to_mate(i):
        return pltpu.make_async_remote_copy(
            src_ref=tx_pair.at[i],
            dst_ref=rx_pair.at[i],
            send_sem=pair_send.at[i],
            recv_sem=pair_recv.at[i],
            device_id=(me, mate),
            device_id_type=MESH,
        )

    def to_far(j, c):
        i = (j - 1) * chunks + c
        return pltpu.make_async_remote_copy(
            src_ref=tx_far.at[i],
            dst_ref=rx_far.at[i],
            send_sem=far_send.at[i],
            recv_sem=far_recv.at[i],
            device_id=(me, 2 * pair_at(j) + side),
            device_id_type=MESH,
        )

    lag = min(2, chunks)
    for j in order:
        for t in range(chunks + lag):
            if t < chunks:
                i = j * chunks + t
                tx_pair[i] = project(j, True, t).astype(jnp.bfloat16)
                to_mate(i).start()
            if t < lag:
                continue
            c = t - lag
            i = j * chunks + c
            mine = project(j, False, c)
            to_mate(i).wait_recv()
            mine = mine + rx_pair[i].astype(jnp.float32)
            if j > 0:
                tx_far[(j - 1) * chunks + c] = mine.astype(jnp.bfloat16)
                to_far(j, c).start()
            else:
                acc[c] = mine
    res_copy.wait()
    out_copies = []
    for c in range(chunks):
        columns = slice(c * width, (c + 1) * width)
        whole = acc[c] + res[:, columns].astype(jnp.float32)
        for j in range(1, pairs):
            to_far(j, c).wait_recv()
            whole = whole + rx_far[(j - 1) * chunks + c].astype(jnp.float32)
        res[:, columns] = whole.astype(res.dtype)
        out_copies.append(
            pltpu.make_async_copy(
                res.at[:, columns], out_hbm.at[:, columns], out_sem.at[c]
            )
        )
        out_copies[c].start()

    for copy in out_copies:
        copy.wait()
    for i in range(pairs * chunks):
        to_mate(i).wait_send()
    for j in range(1, pairs):
        for c in range(chunks):
            to_far(j, c).wait_send()

    def sent(k):
        @pl.when((me + 2 < n_ctx) & (me - (k - 2) >= 0))
        def _():
            for copy in both(direct_part, k):
                copy.wait_send()

        @pl.when((me - k >= 0) & ((odd == 1) | (k < far)))
        def _():
            for copy in both(passed_part, k, k - 1):
                copy.wait_send()

    each(evens, sent)

    @pl.when(odd == 0)
    def _():
        for copy in both(passed_part, 0, 1):
            copy.wait_send()


def local(queries, keys, values, segments, residual, out_weight):
    n_ctx, n_head = lax.axis_size("ctx"), lax.axis_size("head")
    rows, out_cols = residual.shape
    depth = out_weight.shape[0]
    far = n_ctx // 2
    pairs = n_head // 2
    width = min(512, out_cols)
    chunks = out_cols // width
    hbm = pl.BlockSpec(memory_space=pl.ANY)
    bf16 = jnp.bfloat16
    far_slots = max(1, (pairs - 1) * chunks)
    return pl.pallas_call(
        functools.partial(kernel, (n_ctx, n_head, far, chunks)),
        out_shape=jax.ShapeDtypeStruct((rows, out_cols), bf16),
        in_specs=[hbm] * 6,
        out_specs=hbm,
        scratch_shapes=[
            pltpu.VMEM(queries.shape, bf16),
            pltpu.VMEM((n_ctx, rows), jnp.int32),
            pltpu.VMEM((far + 1, 2, rows, HD), bf16),
            pltpu.VMEM((n_head * chunks, depth, width), bf16),
            pltpu.VMEM((pairs * chunks, rows, width), bf16),
            pltpu.VMEM((pairs * chunks, rows, width), bf16),
            pltpu.VMEM((far_slots, rows, width), bf16),
            pltpu.VMEM((far_slots, rows, width), bf16),
            pltpu.VMEM((chunks, rows, width), jnp.float32),
            pltpu.VMEM((rows, out_cols), bf16),
            pltpu.SemaphoreType.DMA((far + 1, 2)),
            pltpu.SemaphoreType.DMA((far + 1, 2)),
            pltpu.SemaphoreType.DMA((far + 1, 2)),
            pltpu.SemaphoreType.DMA((pairs * chunks,)),
            pltpu.SemaphoreType.DMA((pairs * chunks,)),
            pltpu.SemaphoreType.DMA((far_slots,)),
            pltpu.SemaphoreType.DMA((far_slots,)),
            pltpu.SemaphoreType.DMA((n_head * chunks,)),
            pltpu.SemaphoreType.DMA,
            pltpu.SemaphoreType.DMA((chunks,)),
            pltpu.SemaphoreType.DMA((4,)),
        ],
        compiler_params=pltpu.CompilerParams(
            collective_id=0, has_side_effects=True, vmem_limit_bytes=56 * 1024 * 1024
        ),
    )(queries, keys, values, segments.reshape(n_ctx, rows), residual, out_weight)


def solution(mesh):
    placed = (
        P("ctx", "head"),
        P("ctx", "head"),
        P("ctx", "head"),
        P(),
        P("ctx", "head"),
        P("head", None),
    )
    return jax.shard_map(
        local, mesh=mesh, in_specs=placed, out_specs=P("ctx", "head"), check_vma=False
    )
```

```python
import functools
import math

import jax
import jax.numpy as jnp
from jax import lax
from jax.experimental import pallas as pl
from jax.experimental.pallas import tpu as pltpu
from jax.sharding import PartitionSpec as P

HD = 128
MESH = pl.DeviceIdType.MESH


def each(items, body):
    if len(items) <= 8:
        for item in items:
            body(item)
    elif len(items) > 0:

        @pl.loop(0, len(items))
        def _(step):
            body(items.start + step * items.step)


def fold(items, body, state):
    if len(items) <= 8:
        for item in items:
            state = body(item, state)
        return state
    return lax.fori_loop(
        0, len(items), lambda step, s: body(items.start + step * items.step, s), state
    )


def kernel(
    dims,
    q_hbm,
    k_hbm,
    v_hbm,
    seg_hbm,
    res_hbm,
    w_hbm,
    out_hbm,
    q_ref,
    seg_ref,
    kv,
    w,
    tx_pair,
    rx_pair,
    tx_far,
    rx_far,
    acc,
    res,
    kv_send,
    kv_pass,
    kv_recv,
    pair_send,
    pair_recv,
    far_send,
    far_recv,
    w_sem,
    res_sem,
    out_sem,
    in_sem,
):
    n_ctx, n_head, far, chunks = dims
    rows, q_cols = q_ref.shape
    group = q_cols // HD
    out_cols = out_hbm.shape[1]
    width = out_cols // chunks
    pairs = n_head // 2
    me = lax.axis_index("ctx")
    head = lax.axis_index("head")
    side = lax.rem(head, 2)
    pair = lax.div(head, 2)
    mate = head + 1 - 2 * side
    odd = lax.rem(me, 2)
    ctx_mate = me + 1 - 2 * odd

    def pair_at(j):
        return lax.rem(pair + j, pairs)

    barrier = pltpu.get_barrier_semaphore()

    def greet(ctx, hd):
        pl.semaphore_signal(barrier, inc=1, device_id=(ctx, hd), device_id_type=MESH)

    def greet_ctx(k):
        @pl.when(me + k < n_ctx)
        def _():
            greet(me + k, head)

        @pl.when(me - k >= 0)
        def _():
            greet(me - k, head)

    evens = range(2, far + 1, 2)
    greet_ctx(2)
    greet(ctx_mate, head)
    greet(me, mate)
    for j in range(1, pairs):
        greet(me, 2 * pair_at(j) + side)
    inputs = [
        pltpu.make_async_copy(source, target, in_sem.at[i])
        for i, (source, target) in enumerate(
            [
                (k_hbm, kv.at[0, 0]),
                (v_hbm, kv.at[0, 1]),
                (q_hbm, q_ref),
                (seg_hbm, seg_ref),
            ]
        )
    ]
    for copy in inputs:
        copy.start()

    order = [j % pairs for j in range(1, pairs + 1)]

    def w_copy(slot, j, other, c):
        part = 2 * pair_at(j) + (1 - side if other else side)
        start = pl.multiple_of(part * out_cols + c * width, 128)
        return pltpu.make_async_copy(
            w_hbm.at[:, pl.ds(start, width)], w.at[slot], w_sem.at[slot]
        )

    w_copies = {}
    for j in order:
        for c in range(chunks):
            for other in (True, False):
                slot = len(w_copies)
                w_copies[j, other, c] = (slot, w_copy(slot, j, other, c))
    res_copy = pltpu.make_async_copy(res_hbm, res, res_sem)

    def clear(k):
        @pl.when(me - k < 0)
        def _():
            kv[k] = jnp.zeros(kv.shape[1:], kv.dtype)

    each(range(1, far + 1), clear)
    ahead = jnp.where(me + 2 < n_ctx, 1, 0)
    behind = jnp.where(me - 2 >= 0, 1, 0)
    pl.semaphore_wait(barrier, ahead + behind + 1 + pairs)

    inputs[0].wait()
    inputs[1].wait()

    def direct_part(p, k):
        return pltpu.make_async_remote_copy(
            src_ref=kv.at[k - 2, p],
            dst_ref=kv.at[k, p],
            send_sem=kv_send.at[k, p],
            recv_sem=kv_recv.at[k, p],
            device_id=(me + 2, head),
            device_id_type=MESH,
        )

    def passed_part(p, k, lands):
        return pltpu.make_async_remote_copy(
            src_ref=kv.at[k, p],
            dst_ref=kv.at[lands, p],
            send_sem=kv_pass.at[k, p],
            recv_sem=kv_recv.at[lands, p],
            device_id=(ctx_mate, head),
            device_id_type=MESH,
        )

    def arrival_part(p, k):
        return pltpu.make_async_remote_copy(
            src_ref=kv.at[0, p],
            dst_ref=kv.at[k, p],
            send_sem=kv_send.at[k, p],
            recv_sem=kv_recv.at[k, p],
            device_id=(ctx_mate, head),
            device_id_type=MESH,
        )

    def both(make, *args):
        return [make(p, *args) for p in range(2)]

    @pl.when(me + 2 < n_ctx)
    def _():
        for copy in both(direct_part, 2):
            copy.start()

    @pl.when(odd == 0)
    def _():
        for copy in both(passed_part, 0, 1):
            copy.start()

    for _, copy in w_copies.values():
        copy.start()
    res_copy.start()

    inputs[2].wait()
    inputs[3].wait()
    row = lax.broadcasted_iota(jnp.int32, (rows, rows), 0)
    lane = lax.broadcasted_iota(jnp.int32, (rows, rows), 1)
    own_segment = seg_ref[pl.ds(me, 1), :].astype(jnp.float32)
    q_segment = jnp.sum(jnp.where(row == lane, own_segment, 0.0), axis=1, keepdims=True)
    queries = jnp.concatenate([q_ref[:, g * HD : (g + 1) * HD] for g in range(group)], axis=0)
    scale = 1.0 / math.sqrt(HD)

    def attend(k, state):
        best, total, summed = state
        segment = seg_ref[pl.ds(jnp.maximum(me - k, 0), 1), :].astype(jnp.float32)
        near = (lane - k * rows <= row) & (me - k >= 0)
        visible = jnp.where((q_segment == segment) & near, 0.0, -jnp.inf)
        visible = jnp.concatenate([visible] * group, axis=0)
        keys = kv[k, 0]
        values = kv[k, 1]
        scores = lax.dot_general(
            queries, keys, (((1,), (1,)), ((), ())), preferred_element_type=jnp.float32
        )
        scores = scores * scale + visible
        best_new = jnp.maximum(best, jnp.max(scores, axis=1, keepdims=True))
        weights = jnp.exp(scores - best_new)
        shrink = jnp.exp(best - best_new)
        total = total * shrink + jnp.sum(weights, axis=1, keepdims=True)
        summed = summed * shrink + jnp.dot(
            weights.astype(jnp.bfloat16), values, preferred_element_type=jnp.float32
        )
        return best_new, total, summed

    state = (
        jnp.full((group * rows, 1), -1e30, jnp.float32),
        jnp.zeros((group * rows, 1), jnp.float32),
        jnp.zeros((group * rows, HD), jnp.float32),
    )
    state = attend(0, state)

    def take_even(k, state):
        @pl.when(me - k >= 0)
        def _():
            for p in range(2):
                arrival_part(p, k).wait_recv()

                @pl.when((me + 2 < n_ctx) & (k < far))
                def _():
                    direct_part(p, jnp.minimum(k + 2, far)).start()

                @pl.when(odd == 1)
                def _():
                    passed_part(p, k, k - 1).start()

                @pl.when((odd == 0) & (k < far))
                def _():
                    passed_part(p, k, jnp.minimum(k + 1, far)).start()

        return attend(k, state)

    def take_odd(k, state):
        @pl.when(me - k >= 0)
        def _():
            for copy in both(arrival_part, k):
                copy.wait_recv()

        return attend(k, state)

    state = fold(evens, lambda k, s: take_odd(k - 1, take_even(k, s)), state)
    _, total, summed = state
    attended = (summed / total).astype(jnp.bfloat16)
    attended = jnp.concatenate(
        [attended[g * rows : (g + 1) * rows] for g in range(group)], axis=1
    )

    def project(j, other, c):
        slot, copy = w_copies[j, other, c]
        copy.wait()
        return jnp.dot(attended, w[slot], preferred_element_type=jnp.float32)

    def to_mate(i):
        return pltpu.make_async_remote_copy(
            src_ref=tx_pair.at[i],
            dst_ref=rx_pair.at[i],
            send_sem=pair_send.at[i],
            recv_sem=pair_recv.at[i],
            device_id=(me, mate),
            device_id_type=MESH,
        )

    def to_far(j, c):
        i = (j - 1) * chunks + c
        return pltpu.make_async_remote_copy(
            src_ref=tx_far.at[i],
            dst_ref=rx_far.at[i],
            send_sem=far_send.at[i],
            recv_sem=far_recv.at[i],
            device_id=(me, 2 * pair_at(j) + side),
            device_id_type=MESH,
        )

    lag = min(1, chunks)
    for j in order:
        for t in range(chunks + lag):
            if t < chunks:
                i = j * chunks + t
                tx_pair[i] = project(j, True, t).astype(jnp.bfloat16)
                to_mate(i).start()
            if t < lag:
                continue
            c = t - lag
            i = j * chunks + c
            mine = project(j, False, c)
            to_mate(i).wait_recv()
            mine = mine + rx_pair[i].astype(jnp.float32)
            if j > 0:
                tx_far[(j - 1) * chunks + c] = mine.astype(jnp.bfloat16)
                to_far(j, c).start()
            else:
                acc[c] = mine
    res_copy.wait()
    out_copies = []
    for c in range(chunks):
        columns = slice(c * width, (c + 1) * width)
        whole = acc[c] + res[:, columns].astype(jnp.float32)
        for j in range(1, pairs):
            to_far(j, c).wait_recv()
            whole = whole + rx_far[(j - 1) * chunks + c].astype(jnp.float32)
        res[:, columns] = whole.astype(res.dtype)
        out_copies.append(
            pltpu.make_async_copy(
                res.at[:, columns], out_hbm.at[:, columns], out_sem.at[c]
            )
        )
        out_copies[c].start()

    for copy in out_copies:
        copy.wait()
    for i in range(pairs * chunks):
        to_mate(i).wait_send()
    for j in range(1, pairs):
        for c in range(chunks):
            to_far(j, c).wait_send()

    def sent(k):
        @pl.when((me + 2 < n_ctx) & (me - (k - 2) >= 0))
        def _():
            for copy in both(direct_part, k):
                copy.wait_send()

        @pl.when((me - k >= 0) & ((odd == 1) | (k < far)))
        def _():
            for copy in both(passed_part, k, k - 1):
                copy.wait_send()

    each(evens, sent)

    @pl.when(odd == 0)
    def _():
        for copy in both(passed_part, 0, 1):
            copy.wait_send()


def local(queries, keys, values, segments, residual, out_weight):
    n_ctx, n_head = lax.axis_size("ctx"), lax.axis_size("head")
    rows, out_cols = residual.shape
    depth = out_weight.shape[0]
    far = n_ctx // 2
    pairs = n_head // 2
    width = min(512, out_cols)
    chunks = out_cols // width
    hbm = pl.BlockSpec(memory_space=pl.ANY)
    bf16 = jnp.bfloat16
    far_slots = max(1, (pairs - 1) * chunks)
    return pl.pallas_call(
        functools.partial(kernel, (n_ctx, n_head, far, chunks)),
        out_shape=jax.ShapeDtypeStruct((rows, out_cols), bf16),
        in_specs=[hbm] * 6,
        out_specs=hbm,
        scratch_shapes=[
            pltpu.VMEM(queries.shape, bf16),
            pltpu.VMEM((n_ctx, rows), jnp.int32),
            pltpu.VMEM((far + 1, 2, rows, HD), bf16),
            pltpu.VMEM((n_head * chunks, depth, width), bf16),
            pltpu.VMEM((pairs * chunks, rows, width), bf16),
            pltpu.VMEM((pairs * chunks, rows, width), bf16),
            pltpu.VMEM((far_slots, rows, width), bf16),
            pltpu.VMEM((far_slots, rows, width), bf16),
            pltpu.VMEM((chunks, rows, width), jnp.float32),
            pltpu.VMEM((rows, out_cols), bf16),
            pltpu.SemaphoreType.DMA((far + 1, 2)),
            pltpu.SemaphoreType.DMA((far + 1, 2)),
            pltpu.SemaphoreType.DMA((far + 1, 2)),
            pltpu.SemaphoreType.DMA((pairs * chunks,)),
            pltpu.SemaphoreType.DMA((pairs * chunks,)),
            pltpu.SemaphoreType.DMA((far_slots,)),
            pltpu.SemaphoreType.DMA((far_slots,)),
            pltpu.SemaphoreType.DMA((n_head * chunks,)),
            pltpu.SemaphoreType.DMA,
            pltpu.SemaphoreType.DMA((chunks,)),
            pltpu.SemaphoreType.DMA((4,)),
        ],
        compiler_params=pltpu.CompilerParams(
            collective_id=0, has_side_effects=True, vmem_limit_bytes=56 * 1024 * 1024
        ),
    )(queries, keys, values, segments.reshape(n_ctx, rows), residual, out_weight)


def solution(mesh):
    placed = (
        P("ctx", "head"),
        P("ctx", "head"),
        P("ctx", "head"),
        P(),
        P("ctx", "head"),
        P("head", None),
    )
    return jax.shard_map(
        local, mesh=mesh, in_specs=placed, out_specs=P("ctx", "head"), check_vma=False
    )
```

```python
import functools
import math

import jax
import jax.numpy as jnp
from jax import lax
from jax.experimental import pallas as pl
from jax.experimental.pallas import tpu as pltpu
from jax.sharding import PartitionSpec as P

HD = 128
MESH = pl.DeviceIdType.MESH


def each(items, body):
    if len(items) <= 8:
        for item in items:
            body(item)
    elif len(items) > 0:

        @pl.loop(0, len(items))
        def _(step):
            body(items.start + step * items.step)


def fold(items, body, state):
    if len(items) <= 8:
        for item in items:
            state = body(item, state)
        return state
    return lax.fori_loop(
        0, len(items), lambda step, s: body(items.start + step * items.step, s), state
    )


def kernel(
    dims,
    q_hbm,
    k_hbm,
    v_hbm,
    seg_hbm,
    res_hbm,
    w_hbm,
    out_hbm,
    q_ref,
    seg_ref,
    kv,
    w,
    tx_pair,
    rx_pair,
    tx_far,
    rx_far,
    acc,
    res,
    kv_send,
    kv_pass,
    kv_recv,
    pair_send,
    pair_recv,
    far_send,
    far_recv,
    w_sem,
    res_sem,
    out_sem,
    in_sem,
):
    n_ctx, n_head, far, chunks = dims
    rows, q_cols = q_ref.shape
    group = q_cols // HD
    out_cols = out_hbm.shape[1]
    width = out_cols // chunks
    pairs = n_head // 2
    me = lax.axis_index("ctx")
    head = lax.axis_index("head")
    side = lax.rem(head, 2)
    pair = lax.div(head, 2)
    mate = head + 1 - 2 * side
    odd = lax.rem(me, 2)
    ctx_mate = me + 1 - 2 * odd

    def pair_at(j):
        return lax.rem(pair + j, pairs)

    barrier = pltpu.get_barrier_semaphore()

    def greet(ctx, hd):
        pl.semaphore_signal(barrier, inc=1, device_id=(ctx, hd), device_id_type=MESH)

    def greet_ctx(k):
        @pl.when(me + k < n_ctx)
        def _():
            greet(me + k, head)

        @pl.when(me - k >= 0)
        def _():
            greet(me - k, head)

    evens = range(2, far + 1, 2)
    greet_ctx(2)
    greet(ctx_mate, head)
    greet(me, mate)
    for j in range(1, pairs):
        greet(me, 2 * pair_at(j) + side)
    inputs = [
        pltpu.make_async_copy(source, target, in_sem.at[i])
        for i, (source, target) in enumerate(
            [
                (k_hbm.at[: rows // 2], kv.at[0, 0]),
                (k_hbm.at[rows // 2 :], kv.at[0, 1]),
                (v_hbm.at[: rows // 2], kv.at[0, 2]),
                (v_hbm.at[rows // 2 :], kv.at[0, 3]),
                (q_hbm, q_ref),
                (seg_hbm, seg_ref),
            ]
        )
    ]
    for copy in inputs:
        copy.start()

    order = [j % pairs for j in range(1, pairs + 1)]

    def w_copy(slot, j, other, c):
        part = 2 * pair_at(j) + (1 - side if other else side)
        start = pl.multiple_of(part * out_cols + c * width, 128)
        return pltpu.make_async_copy(
            w_hbm.at[:, pl.ds(start, width)], w.at[slot], w_sem.at[slot]
        )

    w_copies = {}
    for j in order:
        for c in range(chunks):
            for other in (True, False):
                slot = len(w_copies)
                w_copies[j, other, c] = (slot, w_copy(slot, j, other, c))
    res_copy = pltpu.make_async_copy(res_hbm, res, res_sem)

    def clear(k):
        @pl.when(me - k < 0)
        def _():
            kv[k] = jnp.zeros(kv.shape[1:], kv.dtype)

    each(range(1, far + 1), clear)
    ahead = jnp.where(me + 2 < n_ctx, 1, 0)
    behind = jnp.where(me - 2 >= 0, 1, 0)
    pl.semaphore_wait(barrier, ahead + behind + 1 + pairs)

    for copy in inputs[:4]:
        copy.wait()

    def direct_part(p, k):
        return pltpu.make_async_remote_copy(
            src_ref=kv.at[k - 2, p],
            dst_ref=kv.at[k, p],
            send_sem=kv_send.at[k, p],
            recv_sem=kv_recv.at[k, p],
            device_id=(me + 2, head),
            device_id_type=MESH,
        )

    def passed_part(p, k, lands):
        return pltpu.make_async_remote_copy(
            src_ref=kv.at[k, p],
            dst_ref=kv.at[lands, p],
            send_sem=kv_pass.at[k, p],
            recv_sem=kv_recv.at[lands, p],
            device_id=(ctx_mate, head),
            device_id_type=MESH,
        )

    def arrival_part(p, k):
        return pltpu.make_async_remote_copy(
            src_ref=kv.at[0, p],
            dst_ref=kv.at[k, p],
            send_sem=kv_send.at[k, p],
            recv_sem=kv_recv.at[k, p],
            device_id=(ctx_mate, head),
            device_id_type=MESH,
        )

    def both(make, *args):
        return [make(p, *args) for p in range(4)]

    @pl.when(me + 2 < n_ctx)
    def _():
        for copy in both(direct_part, 2):
            copy.start()

    @pl.when(odd == 0)
    def _():
        for copy in both(passed_part, 0, 1):
            copy.start()

    for _, copy in w_copies.values():
        copy.start()
    res_copy.start()

    inputs[4].wait()
    inputs[5].wait()
    row = lax.broadcasted_iota(jnp.int32, (rows, rows), 0)
    lane = lax.broadcasted_iota(jnp.int32, (rows, rows), 1)
    own_segment = seg_ref[pl.ds(me, 1), :].astype(jnp.float32)
    q_segment = jnp.sum(jnp.where(row == lane, own_segment, 0.0), axis=1, keepdims=True)
    queries = jnp.concatenate([q_ref[:, g * HD : (g + 1) * HD] for g in range(group)], axis=0)
    scale = 1.0 / math.sqrt(HD)

    def attend(k, state):
        best, total, summed = state
        segment = seg_ref[pl.ds(jnp.maximum(me - k, 0), 1), :].astype(jnp.float32)
        near = (lane - k * rows <= row) & (me - k >= 0)
        visible = jnp.where((q_segment == segment) & near, 0.0, -jnp.inf)
        visible = jnp.concatenate([visible] * group, axis=0)
        keys = kv[k, :2].reshape(rows, HD)
        values = kv[k, 2:].reshape(rows, HD)
        scores = lax.dot_general(
            queries, keys, (((1,), (1,)), ((), ())), preferred_element_type=jnp.float32
        )
        scores = scores * scale + visible
        best_new = jnp.maximum(best, jnp.max(scores, axis=1, keepdims=True))
        weights = jnp.exp(scores - best_new)
        shrink = jnp.exp(best - best_new)
        total = total * shrink + jnp.sum(weights, axis=1, keepdims=True)
        summed = summed * shrink + jnp.dot(
            weights.astype(jnp.bfloat16), values, preferred_element_type=jnp.float32
        )
        return best_new, total, summed

    state = (
        jnp.full((group * rows, 1), -1e30, jnp.float32),
        jnp.zeros((group * rows, 1), jnp.float32),
        jnp.zeros((group * rows, HD), jnp.float32),
    )
    state = attend(0, state)

    def take_even(k, state):
        @pl.when(me - k >= 0)
        def _():
            for p in range(4):
                arrival_part(p, k).wait_recv()

                @pl.when((me + 2 < n_ctx) & (k < far))
                def _():
                    direct_part(p, jnp.minimum(k + 2, far)).start()

                @pl.when(odd == 1)
                def _():
                    passed_part(p, k, k - 1).start()

                @pl.when((odd == 0) & (k < far))
                def _():
                    passed_part(p, k, jnp.minimum(k + 1, far)).start()

        return attend(k, state)

    def take_odd(k, state):
        @pl.when(me - k >= 0)
        def _():
            for copy in both(arrival_part, k):
                copy.wait_recv()

        return attend(k, state)

    state = fold(evens, lambda k, s: take_odd(k - 1, take_even(k, s)), state)
    _, total, summed = state
    attended = (summed / total).astype(jnp.bfloat16)
    attended = jnp.concatenate(
        [attended[g * rows : (g + 1) * rows] for g in range(group)], axis=1
    )

    def project(j, other, c):
        slot, copy = w_copies[j, other, c]
        copy.wait()
        return jnp.dot(attended, w[slot], preferred_element_type=jnp.float32)

    def to_mate(i):
        return pltpu.make_async_remote_copy(
            src_ref=tx_pair.at[i],
            dst_ref=rx_pair.at[i],
            send_sem=pair_send.at[i],
            recv_sem=pair_recv.at[i],
            device_id=(me, mate),
            device_id_type=MESH,
        )

    def to_far(j, c):
        i = (j - 1) * chunks + c
        return pltpu.make_async_remote_copy(
            src_ref=tx_far.at[i],
            dst_ref=rx_far.at[i],
            send_sem=far_send.at[i],
            recv_sem=far_recv.at[i],
            device_id=(me, 2 * pair_at(j) + side),
            device_id_type=MESH,
        )

    lag = min(1, chunks)
    for j in order:
        for t in range(chunks + lag):
            if t < chunks:
                i = j * chunks + t
                tx_pair[i] = project(j, True, t).astype(jnp.bfloat16)
                to_mate(i).start()
            if t < lag:
                continue
            c = t - lag
            i = j * chunks + c
            mine = project(j, False, c)
            to_mate(i).wait_recv()
            mine = mine + rx_pair[i].astype(jnp.float32)
            if j > 0:
                tx_far[(j - 1) * chunks + c] = mine.astype(jnp.bfloat16)
                to_far(j, c).start()
            else:
                acc[c] = mine
    res_copy.wait()
    out_copies = []
    for c in range(chunks):
        columns = slice(c * width, (c + 1) * width)
        whole = acc[c] + res[:, columns].astype(jnp.float32)
        for j in range(1, pairs):
            to_far(j, c).wait_recv()
            whole = whole + rx_far[(j - 1) * chunks + c].astype(jnp.float32)
        res[:, columns] = whole.astype(res.dtype)
        out_copies.append(
            pltpu.make_async_copy(
                res.at[:, columns], out_hbm.at[:, columns], out_sem.at[c]
            )
        )
        out_copies[c].start()

    for copy in out_copies:
        copy.wait()
    for i in range(pairs * chunks):
        to_mate(i).wait_send()
    for j in range(1, pairs):
        for c in range(chunks):
            to_far(j, c).wait_send()

    def sent(k):
        @pl.when((me + 2 < n_ctx) & (me - (k - 2) >= 0))
        def _():
            for copy in both(direct_part, k):
                copy.wait_send()

        @pl.when((me - k >= 0) & ((odd == 1) | (k < far)))
        def _():
            for copy in both(passed_part, k, k - 1):
                copy.wait_send()

    each(evens, sent)

    @pl.when(odd == 0)
    def _():
        for copy in both(passed_part, 0, 1):
            copy.wait_send()


def local(queries, keys, values, segments, residual, out_weight):
    n_ctx, n_head = lax.axis_size("ctx"), lax.axis_size("head")
    rows, out_cols = residual.shape
    depth = out_weight.shape[0]
    far = n_ctx // 2
    pairs = n_head // 2
    width = min(512, out_cols)
    chunks = out_cols // width
    hbm = pl.BlockSpec(memory_space=pl.ANY)
    bf16 = jnp.bfloat16
    far_slots = max(1, (pairs - 1) * chunks)
    return pl.pallas_call(
        functools.partial(kernel, (n_ctx, n_head, far, chunks)),
        out_shape=jax.ShapeDtypeStruct((rows, out_cols), bf16),
        in_specs=[hbm] * 6,
        out_specs=hbm,
        scratch_shapes=[
            pltpu.VMEM(queries.shape, bf16),
            pltpu.VMEM((n_ctx, rows), jnp.int32),
            pltpu.VMEM((far + 1, 4, rows // 2, HD), bf16),
            pltpu.VMEM((n_head * chunks, depth, width), bf16),
            pltpu.VMEM((pairs * chunks, rows, width), bf16),
            pltpu.VMEM((pairs * chunks, rows, width), bf16),
            pltpu.VMEM((far_slots, rows, width), bf16),
            pltpu.VMEM((far_slots, rows, width), bf16),
            pltpu.VMEM((chunks, rows, width), jnp.float32),
            pltpu.VMEM((rows, out_cols), bf16),
            pltpu.SemaphoreType.DMA((far + 1, 4)),
            pltpu.SemaphoreType.DMA((far + 1, 4)),
            pltpu.SemaphoreType.DMA((far + 1, 4)),
            pltpu.SemaphoreType.DMA((pairs * chunks,)),
            pltpu.SemaphoreType.DMA((pairs * chunks,)),
            pltpu.SemaphoreType.DMA((far_slots,)),
            pltpu.SemaphoreType.DMA((far_slots,)),
            pltpu.SemaphoreType.DMA((n_head * chunks,)),
            pltpu.SemaphoreType.DMA,
            pltpu.SemaphoreType.DMA((chunks,)),
            pltpu.SemaphoreType.DMA((6,)),
        ],
        compiler_params=pltpu.CompilerParams(
            collective_id=0, has_side_effects=True, vmem_limit_bytes=56 * 1024 * 1024
        ),
    )(queries, keys, values, segments.reshape(n_ctx, rows), residual, out_weight)


def solution(mesh):
    placed = (
        P("ctx", "head"),
        P("ctx", "head"),
        P("ctx", "head"),
        P(),
        P("ctx", "head"),
        P("head", None),
    )
    return jax.shard_map(
        local, mesh=mesh, in_specs=placed, out_specs=P("ctx", "head"), check_vma=False
    )
```
